32 devices in a mesh: groups: 2 (over y), blk: 4 (over z), dim: 4 (over x, core).
Axes of the slice: x: 2, y: 2, z: 4, core: 2. Of those that a mesh axis runs over, the one named last changes fastest.
Arguments:
- gradients: bfloat16 [2, 2816, 8192], P(None, ('groups', 'blk'), 'dim'), parts along dimension 1, may hold values from -0.65625 to 0.65625
- example_ids: int32 [2816], P(('groups', 'blk')), parts along dimension 0, may hold values from 0 to 1407
- lr_weights: float32 [2], replicated, may hold values from 0.3 to 3
- checkpoint_order: int32 [2], replicated, may hold values from 0 to 1, each once
Outputs:
- scores: float32 [2816, 1408], P(('groups', 'blk', 'dim')), parts along dimension 0
The draws below stay inside these ranges and needn't reach their ends.
There are 2 independent parts, one for each index of `groups`. The reference program is written for one: setup_inputs(seed, part) draws one part's arguments, and reference() takes and returns one part's arrays. A program takes and returns all parts, laid end to end along the dimension named above; an argument that names none is the same for every part. Nothing has to cross between parts.
Inputs may be any that keep to these rules, and one draw needn't show every extreme that they name: `checkpoint_order`: each checkpoint index appears once.
All inputs are finite; a program needn't handle non-finite values.
Results may differ from the reference program's by a relative error of at most 0.008.
Values may be sent and summed in bfloat16 or wider, within the bound.
A program may use at most 64 MiB of HBM per device.

```python
import math
import jax
import jax.numpy as jnp
import numpy as np
from jax import lax

C = 2
F = 8192
EXAMPLES = 1408
N_DIM = 4


def plant(drawn, rng, low, top_value):
    spot = [jax.random.randint(jax.random.fold_in(rng, axis), (), 0, length) for axis, length in enumerate(drawn.shape)]
    widest = drawn.shape.index(max(drawn.shape))
    next_to = spot[:widest] + [(spot[widest] + 1) % drawn.shape[widest]] + spot[widest + 1:]
    return drawn.at[tuple(spot)].set(low).at[tuple(next_to)].set(top_value)


def block_levels(key, extent, shards, low, largest):
    factor_of, own = 1.0, jax.random.fold_in(key, 6)
    for dim, parts in shards:
        steps = jnp.exp(jax.random.uniform(jax.random.fold_in(own, dim), (parts,), jnp.float32, low / len(shards), largest / len(shards)))
        factor_of = factor_of * jnp.repeat(steps, extent[dim] // parts).reshape([-1 if axis == dim else 1 for axis in range(len(extent))])
    return factor_of


def cumulative_ranks(number_of, slope):
    loads = [(1 << 20) // math.isqrt(rank ** slope) + 1 for rank in range(1, number_of + 1)]
    scale = 1 + sum(loads) // (1 << 30)
    return np.cumsum(np.array([max(1, weight // scale) for weight in loads]))


def ranked_ids(key, dims, number_of, lean):
    table = cumulative_ranks(number_of, lean)
    pick = jax.random.randint(jax.random.fold_in(key, 1), dims, 0, int(table[number_of - 1]))
    standing = jnp.searchsorted(jnp.asarray(table, jnp.int32), pick, side="right")
    return jax.random.permutation(jax.random.fold_in(key, 2), number_of)[standing].astype(jnp.int32)


def noise(stream_key, shape, scale, bound, split=(), held_as=jnp.bfloat16):
    level = block_levels(stream_key, shape, split, -0.22, 0.18) if split else 1.0
    drawn = jax.random.normal(stream_key, shape, jnp.float32) * scale * level
    return jnp.minimum(jnp.maximum(drawn, -bound), bound).astype(held_as)


def setup_inputs(seed: int = 0, part: int = 0) -> dict:
    key_list = jax.random.split(jax.random.key(seed), 5)
    part_splits = jax.random.split(jax.random.fold_in(key_list[4], part), 5)
    return {
        "gradients": noise(part_splits[0], (C, EXAMPLES, F), 0.11, 0.65625, ((1, 4), (2, 4))),
        "example_ids": plant(ranked_ids(part_splits[1], (EXAMPLES,), EXAMPLES, 2), jax.random.fold_in(part_splits[1], 3), 0, EXAMPLES - 1).astype(jnp.int32),
        "lr_weights": jnp.clip(jnp.exp(jax.random.uniform(key_list[2], (C,), jnp.float32, math.log(0.3), math.log(3.0))), 0.3, 3.0),
        "checkpoint_order": jax.random.permutation(key_list[3], C).astype(jnp.int32),
    }


def reference(gradients, example_ids, lr_weights, checkpoint_order):
    weights = lr_weights[checkpoint_order]
    width = F // N_DIM
    total = jnp.zeros((EXAMPLES, EXAMPLES), jnp.float32)
    for piece in range(N_DIM):
        partial_sum = jnp.zeros((EXAMPLES, EXAMPLES), jnp.float32)
        for slot in range(C):
            grads = gradients[slot][:, piece * width:(piece + 1) * width]
            partial_sum = partial_sum + weights[slot] * jnp.dot(grads, grads.T, preferred_element_type=jnp.float32)
        rounded = lax.optimization_barrier(partial_sum.astype(jnp.bfloat16))
        total = total + rounded.astype(jnp.float32)
    same = example_ids[:, None] == example_ids[None, :]
    return jnp.where(same, jnp.float32(0.0), total)
```

```python
import functools

import jax
import jax.numpy as jnp
from jax import lax
from jax.experimental import pallas as pl
from jax.experimental.pallas import tpu as pltpu
from jax.sharding import PartitionSpec as P

F32, BF16 = jnp.float32, jnp.bfloat16


def passed_along(value, axis, steps):
    count = lax.axis_size(axis)
    pairs = [(source, (source + steps) % count) for source in range(count)]
    return lax.ppermute(value, axis, pairs)


def tile_term(local, remote, weights):
    products = lax.dot_general(
        local, remote, (((2,), (2,)), ((0,), (0,))), preferred_element_type=jnp.float32
    )
    return jnp.sum(weights[:, None, None] * products, axis=0).astype(jnp.bfloat16)


def place(totals, col_ids, block, ids, anchor, panel, nblk):
    start = jnp.mod(anchor, nblk) * panel
    totals = lax.dynamic_update_slice(totals, block, (jnp.int32(0), start))
    col_ids = lax.dynamic_update_slice(col_ids, ids.astype(jnp.int32), (start,))
    return (totals, col_ids)


def ring_body(gradients, example_ids, lr_weights, checkpoint_order):
    slots = gradients.shape[0]
    panel = gradients.shape[1]
    nblk = lax.axis_size("blk")
    ndim = lax.axis_size("dim")
    rows = panel // ndim
    whole = panel * nblk
    slot_index = jnp.arange(slots, dtype=jnp.int32)
    weights = jnp.sum(
        jnp.where(
            checkpoint_order[:, None] == slot_index[None, :], lr_weights[None, :], jnp.float32(0.0)
        ),
        axis=1,
    )
    mine = lax.axis_index("blk")
    totals = jnp.zeros((rows, whole), jnp.float32)
    col_ids = jnp.zeros((whole,), jnp.int32)

    def direct(remote):
        return lax.psum_scatter(
            tile_term(gradients, remote, weights), "dim", scatter_dimension=0, tiled=True
        ).astype(jnp.float32)

    totals, col_ids = place(totals, col_ids, direct(gradients), example_ids, mine, panel, nblk)

    def advance(step, carry):
        current, current_ids, totals, col_ids = carry
        current, current_ids = passed_along((current, current_ids), "blk", 1)
        totals, col_ids = place(
            totals, col_ids, direct(current), current_ids, mine - step, panel, nblk
        )
        return (current, current_ids, totals, col_ids)

    carry = lax.fori_loop(1, nblk, advance, (gradients, example_ids, totals, col_ids))
    totals, col_ids = (carry[2], carry[3])
    row_ids = lax.dynamic_slice_in_dim(example_ids, lax.axis_index("dim") * rows, rows)
    same = row_ids[:, None] == col_ids[None, :]
    return jnp.where(same, jnp.float32(0.0), totals)


FA, FB, NEAR_T, NEAR_2, ID_N, ID_FA, ID_FB = range(7)
CORE, CROSS, ZED = 7, 14, 21
COPIES = 25
T_FA, T_FB, T_N, T_B, DIAG, N_N, N_B = range(7)


def dot_t(a, b):
    return lax.dot_general(a, b, (((1,), (1,)), ((), ())), preferred_element_type=F32)


def kernel(
    g, ids, lr, order, out_d, out_n, out_f, out_ids,
    gv, oside, fbuf, near2, idbuf,
    acc_w, cs_w, cr_w, xs_w, xr_w, zs_w, zr_w,
    acc_s, cs_s, cr_s, xs_s, xr_s, zs_s, zr_s,
    send, recv, local,
):
    b, d = lax.axis_index("blk"), lax.axis_index("dim")
    bp, ct = lax.rem(b, 2), b // 2
    near = b + 1 - 2 * bp
    fa, fb = lax.rem(b + 2, 4), lax.rem(near + 2, 4)
    c, x = lax.rem(d, 2), d // 2
    core, cross = d + 1 - 2 * c, lax.rem(d + 2, 4)
    panel, feat = g.shape[1], g.shape[2]
    half, rows = feat // 2, panel // 4

    def cols(p):
        return pl.ds(pl.multiple_of(p * half, 128), half)

    loads = [
        pltpu.make_async_copy(g, gv, local.at[0]),
        pltpu.make_async_copy(g.at[ct, :, cols(bp)], oside.at[bp], local.at[1]),
        pltpu.make_async_copy(ids, idbuf.at[b], local.at[2]),
    ]
    for load in loads:
        load.start()

    barrier = pltpu.get_barrier_semaphore()
    for target in ({"blk": near}, {"blk": fa}, {"blk": fb}, {"dim": core}, {"dim": cross}):
        pl.semaphore_signal(barrier, inc=1, device_id=target, device_id_type=pl.DeviceIdType.MESH)
    pl.semaphore_wait(barrier, 5)

    def remote(src, dst, k, target):
        copy = pltpu.make_async_remote_copy(
            src_ref=src, dst_ref=dst, send_sem=send.at[k], recv_sem=recv.at[k],
            device_id=target, device_id_type=pl.DeviceIdType.MESH,
        )
        copy.start()
        return copy

    flight = {}
    flight[FB] = remote(g.at[1 - ct, :, cols(1 - bp)], fbuf.at[bp], FB, {"blk": fb})
    flight[FA] = remote(g.at[1 - ct, :, cols(bp)], fbuf.at[bp], FA, {"blk": fa})
    flight[NEAR_T] = remote(g.at[ct, :, cols(1 - bp)], oside.at[bp], NEAR_T, {"blk": near})
    flight[NEAR_2] = remote(g.at[1 - ct, :, cols(1 - bp)], near2, NEAR_2, {"blk": near})
    for k, to in ((ID_N, near), (ID_FA, fa), (ID_FB, fb)):
        flight[k] = remote(ids, idbuf.at[b], k, {"blk": to})

    def weight(slot):
        total = jnp.float32(0.0)
        for k in range(lr.shape[0]):
            total = total + jnp.where(order[slot] == k, lr[k], jnp.float32(0.0))
        return total

    w0, w1 = weight(0), weight(1)
    w_t = jnp.where(ct == 0, w0, w1)
    w_o = jnp.where(ct == 0, w1, w0)

    def bufs(r):
        if r < DIAG:
            return r, acc_w, cs_w, cr_w, xs_w, xr_w
        return r - DIAG, acc_s, cs_s, cr_s, xs_s, xr_s

    def to_core(r, value):
        i, acc, cs, cr, _, _ = bufs(r)
        for q in range(4):
            acc[i, q] = value[q * rows:(q + 1) * rows]
        for q in range(2):
            cs[i, q] = acc[i, 2 * q + 1 - c].astype(BF16)
        flight[CORE + r] = remote(cs.at[i], cr.at[i], CORE + r, {"dim": core})

    def to_cross(r):
        i, acc, _, cr, xs, xr = bufs(r)
        flight[CORE + r].wait_recv()
        y = 1 - x
        xs[i] = (acc[i, 2 * y + c] + cr[i, y].astype(F32)).astype(BF16)
        flight[CROSS + r] = remote(xs.at[i], xr.at[i], CROSS + r, {"dim": cross})

    def summed(r):
        i, acc, _, cr, _, xr = bufs(r)
        flight[CROSS + r].wait_recv()
        return acc[i, 2 * x + c] + cr[i, x].astype(F32) + xr[i].astype(F32)

    for load in loads:
        load.wait()
    to_core(DIAG, w0 * dot_t(gv[0], gv[0]) + w1 * dot_t(gv[1], gv[1]))
    to_cross(DIAG)
    out_d[...] = summed(DIAG)

    flight[NEAR_T].wait_recv()
    flight[NEAR_2].wait_recv()
    own2 = gv[1 - ct, :, cols(bp)]
    to_core(N_N, w_t * dot_t(oside[1 - bp], oside[bp]) + w_o * dot_t(near2[...], own2))
    to_core(N_B, w_t * dot_t(oside[bp], oside[1 - bp]) + w_o * dot_t(own2, near2[...]))
    to_cross(N_N)
    to_cross(N_B)
    zs_s[...] = summed(N_N).astype(BF16)
    flight[ZED + 3] = remote(zs_s, zr_s, ZED + 3, {"blk": near})
    n_own = summed(N_B)
    flight[ZED + 3].wait_recv()
    out_n[...] = n_own + zr_s[...].astype(F32)

    flight[FA].wait_recv()
    flight[FB].wait_recv()
    side = oside[...].reshape(2 * panel, half)
    far = fbuf[...].reshape(2 * panel, half)
    to_core(T_FA, w_t * dot_t(fbuf[bp], side))
    to_core(T_FB, w_t * dot_t(fbuf[1 - bp], side))
    to_cross(T_FA)
    to_core(T_N, w_t * dot_t(oside[1 - bp], far))
    to_cross(T_FB)
    to_core(T_B, w_t * dot_t(oside[bp], far))
    to_cross(T_N)
    to_cross(T_B)
    for k, (r, to) in enumerate(((T_FA, fa), (T_FB, fb), (T_N, near))):
        zs_w[k] = summed(r).astype(BF16)
        flight[ZED + k] = remote(zs_w.at[k], zr_w.at[k], ZED + k, {"blk": to})
    total = summed(T_B)
    for k in (2, 0, 1):
        flight[ZED + k].wait_recv()
        total = total + zr_w[k].astype(F32)
    out_f[...] = total
    for k in (ID_N, ID_FA, ID_FB):
        flight[k].wait_recv()
    out_ids[...] = idbuf[...]
    for k in range(COPIES):
        flight[k].wait_send()


def two_level_body(gradients, example_ids, lr_weights, checkpoint_order):
    slots, panel, feat = gradients.shape
    half, rows = feat // 2, panel // 4
    vmem = pl.BlockSpec(memory_space=pltpu.VMEM)
    smem = pl.BlockSpec(memory_space=pltpu.SMEM)

    def partials(count, width):
        return [
            pltpu.VMEM((count, 4, rows, width), F32),
            pltpu.VMEM((count, 2, rows, width), BF16),
            pltpu.VMEM((count, 2, rows, width), BF16),
            pltpu.VMEM((count, rows, width), BF16),
            pltpu.VMEM((count, rows, width), BF16),
        ]

    d_tile, n_tile, f_tile, col_ids = pl.pallas_call(
        kernel,
        out_shape=[
            jax.ShapeDtypeStruct((rows, panel), F32),
            jax.ShapeDtypeStruct((rows, panel), F32),
            jax.ShapeDtypeStruct((rows, 2 * panel), F32),
            jax.ShapeDtypeStruct((4, 1, panel), jnp.int32),
        ],
        in_specs=[pl.BlockSpec(memory_space=pl.ANY), vmem, smem, smem],
        out_specs=[vmem] * 4,
        scratch_shapes=[
            pltpu.VMEM((slots, panel, feat), BF16),
            pltpu.VMEM((2, panel, half), BF16),
            pltpu.VMEM((2, panel, half), BF16),
            pltpu.VMEM((panel, half), BF16),
            pltpu.VMEM((4, 1, panel), jnp.int32),
            *partials(4, 2 * panel),
            pltpu.VMEM((3, rows, 2 * panel), BF16),
            pltpu.VMEM((3, rows, 2 * panel), BF16),
            *partials(3, panel),
            pltpu.VMEM((rows, panel), BF16),
            pltpu.VMEM((rows, panel), BF16),
            pltpu.SemaphoreType.DMA((COPIES,)),
            pltpu.SemaphoreType.DMA((COPIES,)),
            pltpu.SemaphoreType.DMA((3,)),
        ],
        compiler_params=pltpu.CompilerParams(
            collective_id=0, has_side_effects=True, vmem_limit_bytes=48 * 1024 * 1024
        ),
    )(gradients, example_ids.reshape(1, panel), lr_weights, checkpoint_order)

    b = lax.axis_index("blk")
    side = jnp.where(
        lax.rem(b, 2) == 0,
        jnp.concatenate([d_tile, n_tile], axis=1),
        jnp.concatenate([n_tile, d_tile], axis=1),
    )
    totals = jnp.where(
        b < 2,
        jnp.concatenate([side, f_tile], axis=1),
        jnp.concatenate([f_tile, side], axis=1),
    )
    row_ids = lax.dynamic_slice_in_dim(example_ids, lax.axis_index("dim") * rows, rows)
    same = row_ids[:, None] == col_ids.reshape(1, 4 * panel)
    return jnp.where(same, jnp.float32(0.0), totals)


def solution(mesh):
    fits = mesh.shape["blk"] == 4 and mesh.shape["dim"] == 4
    return jax.shard_map(
        two_level_body if fits else ring_body,
        mesh=mesh,
        in_specs=(P(None, ("groups", "blk"), "dim"), P(("groups", "blk")), P(), P()),
        out_specs=P(("groups", "blk", "dim"), None),
        check_vma=False,
    )
```

```python
import functools

import jax
import jax.numpy as jnp
from jax import lax
from jax.experimental import pallas as pl
from jax.experimental.pallas import tpu as pltpu
from jax.sharding import PartitionSpec as P

F32, BF16 = jnp.float32, jnp.bfloat16


def passed_along(value, axis, steps):
    count = lax.axis_size(axis)
    pairs = [(source, (source + steps) % count) for source in range(count)]
    return lax.ppermute(value, axis, pairs)


def tile_term(local, remote, weights):
    products = lax.dot_general(
        local, remote, (((2,), (2,)), ((0,), (0,))), preferred_element_type=jnp.float32
    )
    return jnp.sum(weights[:, None, None] * products, axis=0).astype(jnp.bfloat16)


def place(totals, col_ids, block, ids, anchor, panel, nblk):
    start = jnp.mod(anchor, nblk) * panel
    totals = lax.dynamic_update_slice(totals, block, (jnp.int32(0), start))
    col_ids = lax.dynamic_update_slice(col_ids, ids.astype(jnp.int32), (start,))
    return (totals, col_ids)


def ring_body(gradients, example_ids, lr_weights, checkpoint_order):
    slots = gradients.shape[0]
    panel = gradients.shape[1]
    nblk = lax.axis_size("blk")
    ndim = lax.axis_size("dim")
    rows = panel // ndim
    whole = panel * nblk
    slot_index = jnp.arange(slots, dtype=jnp.int32)
    weights = jnp.sum(
        jnp.where(
            checkpoint_order[:, None] == slot_index[None, :], lr_weights[None, :], jnp.float32(0.0)
        ),
        axis=1,
    )
    mine = lax.axis_index("blk")
    totals = jnp.zeros((rows, whole), jnp.float32)
    col_ids = jnp.zeros((whole,), jnp.int32)

    def direct(remote):
        return lax.psum_scatter(
            tile_term(gradients, remote, weights), "dim", scatter_dimension=0, tiled=True
        ).astype(jnp.float32)

    totals, col_ids = place(totals, col_ids, direct(gradients), example_ids, mine, panel, nblk)

    def advance(step, carry):
        current, current_ids, totals, col_ids = carry
        current, current_ids = passed_along((current, current_ids), "blk", 1)
        totals, col_ids = place(
            totals, col_ids, direct(current), current_ids, mine - step, panel, nblk
        )
        return (current, current_ids, totals, col_ids)

    carry = lax.fori_loop(1, nblk, advance, (gradients, example_ids, totals, col_ids))
    totals, col_ids = (carry[2], carry[3])
    row_ids = lax.dynamic_slice_in_dim(example_ids, lax.axis_index("dim") * rows, rows)
    same = row_ids[:, None] == col_ids[None, :]
    return jnp.where(same, jnp.float32(0.0), totals)


BOUNDS = (40,)
COPIES = 96


def far_chunks(rows):
    chunks, outer = [], rows
    for inner in (*BOUNDS, 0):
        ranges = []
        for pair in range(2):
            middle = (2 * pair + 1) * rows
            if inner:
                ranges += [(middle - outer, middle - inner), (middle + inner, middle + outer)]
            else:
                ranges += [(middle - outer, middle + outer)]
        merged = []
        for low, high in ranges:
            if merged and merged[-1][1] == low:
                merged[-1] = (merged[-1][0], high)
            else:
                merged.append((low, high))
        chunks.append((outer - inner, merged))
        outer = inner
    return chunks


def dot_t(a, b):
    return lax.dot_general(a, b, (((1,), (1,)), ((), ())), preferred_element_type=F32)


def kernel(
    g, ids, lr_in, order_in, out_d, out_n, out_f, out_ids,
    lr, order, gv, oside, near2, idbuf, send, recv, local, *scratch,
):
    b, d = lax.axis_index("blk"), lax.axis_index("dim")
    bp, ct = lax.rem(b, 2), b // 2
    near = b + 1 - 2 * bp
    fa, fb = lax.rem(b + 2, 4), lax.rem(near + 2, 4)
    c, x = lax.rem(d, 2), d // 2
    core, cross = d + 1 - 2 * c, lax.rem(d + 2, 4)
    panel, feat = g.shape[1], g.shape[2]
    half, rows = feat // 2, panel // 4
    chunks = far_chunks(rows)
    groups = [scratch[7 * k:7 * k + 7] for k in range(2 + 2 * len(chunks))]
    fbufs = scratch[7 * len(groups):]

    def cols(p):
        return pl.ds(pl.multiple_of(p * half, 128), half)

    loads = [
        pltpu.make_async_copy(g, gv, local.at[0]),
        pltpu.make_async_copy(g.at[ct, :, cols(bp)], oside.at[bp], local.at[1]),
        pltpu.make_async_copy(ids, idbuf.at[b], local.at[2]),
        pltpu.make_async_copy(lr_in, lr, local.at[3]),
        pltpu.make_async_copy(order_in, order, local.at[4]),
    ]

    barrier = pltpu.get_barrier_semaphore()
    for target in ({"blk": near}, {"blk": fa}, {"blk": fb}, {"dim": core}, {"dim": cross}):
        pl.semaphore_signal(barrier, inc=1, device_id=target, device_id_type=pl.DeviceIdType.MESH)
    pl.semaphore_wait(barrier, 5)

    started = []

    def remote(src, dst, target):
        k = len(started)
        copy = pltpu.make_async_remote_copy(
            src_ref=src, dst_ref=dst, send_sem=send.at[k], recv_sem=recv.at[k],
            device_id=target, device_id_type=pl.DeviceIdType.MESH,
        )
        copy.start()
        started.append(copy)
        return copy

    arriving = []

    def send_far(h):
        count, ranges = chunks[h]
        flight = []
        for to, p in ((fb, 1 - bp), (fa, bp)):
            place_at = 0
            for low, high in ranges:
                flight.append(remote(
                    g.at[1 - ct, pl.ds(low, high - low), cols(p)],
                    fbufs[h].at[bp, pl.ds(place_at, high - low)],
                    {"blk": to},
                ))
                place_at += high - low
        arriving.append(flight)

    send_far(0)
    near_t = remote(g.at[ct, :, cols(1 - bp)], oside.at[bp], {"blk": near})
    for load in loads:
        load.start()
    for load in loads:
        load.wait()
    id_copies = [remote(idbuf.at[b], idbuf.at[b], {"blk": to}) for to in (near, fa, fb)]

    def weight(slot):
        total = jnp.float32(0.0)
        for k in range(lr.shape[0]):
            total = total + jnp.where(order[slot] == k, lr[k], jnp.float32(0.0))
        return total

    w0, w1 = weight(0), weight(1)
    w_t = jnp.where(ct == 0, w0, w1)
    w_o = jnp.where(ct == 0, w1, w0)
    flight = {}

    def to_core(grp, i, value):
        acc, cs, cr = groups[grp][:3]
        height = acc.shape[2]
        for q in range(4):
            acc[i, q] = value[q * height:(q + 1) * height]
        for q in range(2):
            cs[i, q] = acc[i, 2 * q + 1 - c].astype(BF16)
        flight[grp, i, 0] = remote(cs.at[i], cr.at[i], {"dim": core})

    def to_cross(grp, i):
        acc, _, cr, xs, xr = groups[grp][:5]
        flight[grp, i, 0].wait_recv()
        y = 1 - x
        xs[i] = (acc[i, 2 * y + c] + cr[i, y].astype(F32)).astype(BF16)
        flight[grp, i, 1] = remote(xs.at[i], xr.at[i], {"dim": cross})

    def summed(grp, i):
        acc, _, cr, _, xr = groups[grp][:5]
        flight[grp, i, 1].wait_recv()
        return acc[i, 2 * x + c] + cr[i, x].astype(F32) + xr[i].astype(F32)

    def to_zed(grp, i, to):
        zs, zr = groups[grp][5:]
        zs[i] = summed(grp, i).astype(BF16)
        flight[grp, i, 2] = remote(zs.at[i], zr.at[i], {"blk": to})

    def arrived(grp, i):
        flight[grp, i, 2].wait_recv()
        return groups[grp][6][i].astype(F32)

    to_core(0, 0, w0 * dot_t(gv[0], gv[0]) + w1 * dot_t(gv[1], gv[1]))
    to_cross(0, 0)
    out_d[...] = summed(0, 0)

    def near_tiles():
        near_o.wait_recv()
        own2 = gv[1 - ct, :, cols(bp)]
        to_core(1, 0, w_t * dot_t(oside[1 - bp], oside[bp]) + w_o * dot_t(near2[...], own2))
        to_core(1, 1, w_t * dot_t(oside[bp], oside[1 - bp]) + w_o * dot_t(own2, near2[...]))
    def far_tiles(h):
        rowwise, colwise = 2 + 2 * h, 3 + 2 * h
        for copy in arriving[h]:
            copy.wait_recv()
        side = oside[...].reshape(2 * panel, half)
        far = fbufs[h][...].reshape(2 * fbufs[h].shape[1], half)
        last = h == len(chunks) - 1
        to_core(rowwise, 0, w_t * dot_t(fbufs[h][bp], side))
        to_core(rowwise, 1, w_t * dot_t(fbufs[h][1 - bp], side))
        to_cross(rowwise, 0)
        to_core(colwise, 0, w_t * dot_t(oside[1 - bp], far))
        to_cross(rowwise, 1)
        to_core(colwise, 1, w_t * dot_t(oside[bp], far))
        to_cross(colwise, 0)
        to_zed(rowwise, 0, fa)
        to_cross(colwise, 1)
        to_zed(rowwise, 1, fb)
        if last:
            near_tiles()
        to_zed(colwise, 0, near)
        if last:
            to_cross(1, 0)
            to_cross(1, 1)
            to_zed(1, 0, near)

    def finish_cols(h):
        own = summed(3 + 2 * h, 1) + arrived(3 + 2 * h, 0)
        at = 0
        for p in range(2):
            for low, high in chunks[h][1]:
                out_f[:, p * panel + low:p * panel + high] = own[:, at:at + high - low]
                at += high - low

    def finish_rows(h):
        count = chunks[h][0]
        before = sum(chunk[0] for chunk in chunks[:h])
        at = jnp.where(c == 0, before, rows - before - count)
        at = pl.multiple_of(at, 8)
        out_f[pl.ds(at, count)] = out_f[pl.ds(at, count)] + arrived(2 + 2 * h, 0) + arrived(2 + 2 * h, 1)

    near_t.wait_recv()
    left = [near_t]
    for h in range(len(chunks)):
        if h == 0:
            near_t.wait_send()
        if h + 1 < len(chunks):
            for copy in arriving[h]:
                copy.wait_send()
            left += arriving[h]
            if h == 0:
                near_o = remote(g.at[1 - ct, :, cols(1 - bp)], near2, {"blk": near})
            send_far(h + 1)
        if h > 0:
            finish_cols(h - 1)
        far_tiles(h)
    finish_cols(len(chunks) - 1)
    for h in range(len(chunks)):
        finish_rows(h)
    out_n[...] = summed(1, 1) + arrived(1, 0)
    for copy in id_copies:
        copy.wait_recv()
    out_ids[...] = idbuf[...]
    for copy in started:
        if not any(copy is other for other in left):
            copy.wait_send()


def two_level_body(gradients, example_ids, lr_weights, checkpoint_order):
    slots, panel, feat = gradients.shape
    half, rows = feat // 2, panel // 4
    vmem = pl.BlockSpec(memory_space=pltpu.VMEM)
    anywhere = pl.BlockSpec(memory_space=pl.ANY)
    chunks = far_chunks(rows)

    def partials(count, height, width):
        return [
            pltpu.VMEM((count, 4, height, width), F32),
            pltpu.VMEM((count, 2, height, width), BF16),
            pltpu.VMEM((count, 2, height, width), BF16),
            *[pltpu.VMEM((count, height, width), BF16)] * 4,
        ]

    scratch = partials(1, rows, panel) + partials(2, rows, panel)
    for count, _ in chunks:
        scratch += partials(2, count, 2 * panel) + partials(2, rows, 8 * count)
    scratch += [pltpu.VMEM((2, 4 * count, half), BF16) for count, _ in chunks]

    d_tile, n_tile, f_tile, col_ids = pl.pallas_call(
        kernel,
        out_shape=[
            jax.ShapeDtypeStruct((rows, panel), F32),
            jax.ShapeDtypeStruct((rows, panel), F32),
            jax.ShapeDtypeStruct((rows, 2 * panel), F32),
            jax.ShapeDtypeStruct((4, 1, panel), jnp.int32),
        ],
        in_specs=[anywhere] * 4,
        out_specs=[vmem] * 4,
        scratch_shapes=[
            pltpu.SMEM(lr_weights.shape, F32),
            pltpu.SMEM(checkpoint_order.shape, jnp.int32),
            pltpu.VMEM((slots, panel, feat), BF16),
            pltpu.VMEM((2, panel, half), BF16),
            pltpu.VMEM((panel, half), BF16),
            pltpu.VMEM((4, 1, panel), jnp.int32),
            pltpu.SemaphoreType.DMA((COPIES,)),
            pltpu.SemaphoreType.DMA((COPIES,)),
            pltpu.SemaphoreType.DMA((5,)),
            *scratch,
        ],
        compiler_params=pltpu.CompilerParams(
            collective_id=0, has_side_effects=True, vmem_limit_bytes=60 * 1024 * 1024
        ),
    )(gradients, example_ids.reshape(1, panel), lr_weights, checkpoint_order)

    b = lax.axis_index("blk")
    side = jnp.where(
        lax.rem(b, 2) == 0,
        jnp.concatenate([d_tile, n_tile], axis=1),
        jnp.concatenate([n_tile, d_tile], axis=1),
    )
    totals = jnp.where(
        b < 2,
        jnp.concatenate([side, f_tile], axis=1),
        jnp.concatenate([f_tile, side], axis=1),
    )
    row_ids = lax.dynamic_slice_in_dim(example_ids, lax.axis_index("dim") * rows, rows)
    same = row_ids[:, None] == col_ids.reshape(1, 4 * panel)
    return jnp.where(same, jnp.float32(0.0), totals)


def solution(mesh):
    fits = mesh.shape["blk"] == 4 and mesh.shape["dim"] == 4
    return jax.shard_map(
        two_level_body if fits else ring_body,
        mesh=mesh,
        in_specs=(P(None, ("groups", "blk"), "dim"), P(("groups", "blk")), P(), P()),
        out_specs=P(("groups", "blk", "dim"), None),
        check_vma=False,
    )
```

```python
import functools

import jax
import jax.numpy as jnp
from jax import lax
from jax.experimental import pallas as pl
from jax.experimental.pallas import tpu as pltpu
from jax.sharding import PartitionSpec as P

F32, BF16 = jnp.float32, jnp.bfloat16


def passed_along(value, axis, steps):
    count = lax.axis_size(axis)
    pairs = [(source, (source + steps) % count) for source in range(count)]
    return lax.ppermute(value, axis, pairs)


def tile_term(local, remote, weights):
    products = lax.dot_general(
        local, remote, (((2,), (2,)), ((0,), (0,))), preferred_element_type=jnp.float32
    )
    return jnp.sum(weights[:, None, None] * products, axis=0).astype(jnp.bfloat16)


def place(totals, col_ids, block, ids, anchor, panel, nblk):
    start = jnp.mod(anchor, nblk) * panel
    totals = lax.dynamic_update_slice(totals, block, (jnp.int32(0), start))
    col_ids = lax.dynamic_update_slice(col_ids, ids.astype(jnp.int32), (start,))
    return (totals, col_ids)


def ring_body(gradients, example_ids, lr_weights, checkpoint_order):
    slots = gradients.shape[0]
    panel = gradients.shape[1]
    nblk = lax.axis_size("blk")
    ndim = lax.axis_size("dim")
    rows = panel // ndim
    whole = panel * nblk
    slot_index = jnp.arange(slots, dtype=jnp.int32)
    weights = jnp.sum(
        jnp.where(
            checkpoint_order[:, None] == slot_index[None, :], lr_weights[None, :], jnp.float32(0.0)
        ),
        axis=1,
    )
    mine = lax.axis_index("blk")
    totals = jnp.zeros((rows, whole), jnp.float32)
    col_ids = jnp.zeros((whole,), jnp.int32)

    def direct(remote):
        return lax.psum_scatter(
            tile_term(gradients, remote, weights), "dim", scatter_dimension=0, tiled=True
        ).astype(jnp.float32)

    totals, col_ids = place(totals, col_ids, direct(gradients), example_ids, mine, panel, nblk)

    def advance(step, carry):
        current, current_ids, totals, col_ids = carry
        current, current_ids = passed_along((current, current_ids), "blk", 1)
        totals, col_ids = place(
            totals, col_ids, direct(current), current_ids, mine - step, panel, nblk
        )
        return (current, current_ids, totals, col_ids)

    carry = lax.fori_loop(1, nblk, advance, (gradients, example_ids, totals, col_ids))
    totals, col_ids = (carry[2], carry[3])
    row_ids = lax.dynamic_slice_in_dim(example_ids, lax.axis_index("dim") * rows, rows)
    same = row_ids[:, None] == col_ids[None, :]
    return jnp.where(same, jnp.float32(0.0), totals)


BOUNDS = (24,)
EARLY = True
PACE = 1
COPIES = 96


def far_chunks(rows):
    chunks, outer = [], rows
    for inner in (*BOUNDS, 0):
        ranges = []
        for pair in range(2):
            middle = (2 * pair + 1) * rows
            if inner:
                ranges += [(middle - outer, middle - inner), (middle + inner, middle + outer)]
            else:
                ranges += [(middle - outer, middle + outer)]
        merged = []
        for low, high in ranges:
            if merged and merged[-1][1] == low:
                merged[-1] = (merged[-1][0], high)
            else:
                merged.append((low, high))
        chunks.append((outer - inner, merged))
        outer = inner
    return chunks


def dot_t(a, b):
    return lax.dot_general(a, b, (((1,), (1,)), ((), ())), preferred_element_type=F32)


def kernel(
    g, ids, lr_in, order_in, out_d, out_n, out_f, out_ids,
    lr, order, gv, oside, near2, idbuf, send, recv, local, *scratch,
):
    b, d = lax.axis_index("blk"), lax.axis_index("dim")
    bp, ct = lax.rem(b, 2), b // 2
    near = b + 1 - 2 * bp
    fa, fb = lax.rem(b + 2, 4), lax.rem(near + 2, 4)
    c, x = lax.rem(d, 2), d // 2
    core, cross = d + 1 - 2 * c, lax.rem(d + 2, 4)
    panel, feat = g.shape[1], g.shape[2]
    half, rows = feat // 2, panel // 4
    chunks = far_chunks(rows)
    groups = [scratch[7 * k:7 * k + 7] for k in range(2 + 2 * len(chunks))]
    fbufs = scratch[7 * len(groups):]

    def cols(p):
        return pl.ds(pl.multiple_of(p * half, 128), half)

    loads = [
        pltpu.make_async_copy(g, gv, local.at[0]),
        pltpu.make_async_copy(g.at[ct, :, cols(bp)], oside.at[bp], local.at[1]),
        pltpu.make_async_copy(ids, idbuf.at[b], local.at[2]),
        pltpu.make_async_copy(lr_in, lr, local.at[3]),
        pltpu.make_async_copy(order_in, order, local.at[4]),
    ]

    barrier = pltpu.get_barrier_semaphore()
    for target in ({"blk": near}, {"blk": fa}, {"blk": fb}, {"dim": core}, {"dim": cross}):
        pl.semaphore_signal(barrier, inc=1, device_id=target, device_id_type=pl.DeviceIdType.MESH)
    pl.semaphore_wait(barrier, 5)

    started = []

    def remote(src, dst, target):
        k = len(started)
        copy = pltpu.make_async_remote_copy(
            src_ref=src, dst_ref=dst, send_sem=send.at[k], recv_sem=recv.at[k],
            device_id=target, device_id_type=pl.DeviceIdType.MESH,
        )
        copy.start()
        started.append(copy)
        return copy

    arriving = []

    def send_far(h):
        count, ranges = chunks[h]
        flight = []
        for to, p in ((fb, 1 - bp), (fa, bp)):
            place_at = 0
            for low, high in ranges:
                flight.append(remote(
                    g.at[1 - ct, pl.ds(low, high - low), cols(p)],
                    fbufs[h].at[bp, pl.ds(place_at, high - low)],
                    {"blk": to},
                ))
                place_at += high - low
        arriving.append(flight)

    send_far(0)
    near_t = remote(g.at[ct, :, cols(1 - bp)], oside.at[bp], {"blk": near})
    near_o = []

    def send_near(part):
        piece = pl.ds(part * 2 * rows, 2 * rows)
        near_o.append(remote(g.at[1 - ct, piece, cols(1 - bp)], near2.at[piece], {"blk": near}))

    if EARLY:
        send_near(0)
    for load in loads:
        load.start()
    for load in loads:
        load.wait()
    id_copies = [remote(idbuf.at[b], idbuf.at[b], {"blk": to}) for to in (near, fa, fb)]

    def weight(slot):
        total = jnp.float32(0.0)
        for k in range(lr.shape[0]):
            total = total + jnp.where(order[slot] == k, lr[k], jnp.float32(0.0))
        return total

    w0, w1 = weight(0), weight(1)
    w_t = jnp.where(ct == 0, w0, w1)
    w_o = jnp.where(ct == 0, w1, w0)
    flight = {}

    def to_core(grp, i, value):
        acc, cs, cr = groups[grp][:3]
        height = acc.shape[2]
        for q in range(4):
            acc[i, q] = value[q * height:(q + 1) * height]
        for q in range(2):
            cs[i, q] = acc[i, 2 * q + 1 - c].astype(BF16)
        flight[grp, i, 0] = remote(cs.at[i], cr.at[i], {"dim": core})

    def to_cross(grp, i):
        acc, _, cr, xs, xr = groups[grp][:5]
        flight[grp, i, 0].wait_recv()
        y = 1 - x
        xs[i] = (acc[i, 2 * y + c] + cr[i, y].astype(F32)).astype(BF16)
        flight[grp, i, 1] = remote(xs.at[i], xr.at[i], {"dim": cross})

    def summed(grp, i):
        acc, _, cr, _, xr = groups[grp][:5]
        flight[grp, i, 1].wait_recv()
        return acc[i, 2 * x + c] + cr[i, x].astype(F32) + xr[i].astype(F32)

    def to_zed(grp, i, to):
        zs, zr = groups[grp][5:]
        zs[i] = summed(grp, i).astype(BF16)
        flight[grp, i, 2] = remote(zs.at[i], zr.at[i], {"blk": to})

    def arrived(grp, i):
        flight[grp, i, 2].wait_recv()
        return groups[grp][6][i].astype(F32)

    to_core(0, 0, w0 * dot_t(gv[0], gv[0]) + w1 * dot_t(gv[1], gv[1]))

    def near_tiles():
        for copy in near_o:
            copy.wait_recv()
        own2 = gv[1 - ct, :, cols(bp)]
        to_core(1, 0, w_t * dot_t(oside[1 - bp], oside[bp]) + w_o * dot_t(near2[...], own2))
        to_core(1, 1, w_t * dot_t(oside[bp], oside[1 - bp]) + w_o * dot_t(own2, near2[...]))
    def far_tiles(h):
        rowwise, colwise = 2 + 2 * h, 3 + 2 * h
        for copy in arriving[h]:
            copy.wait_recv()
        side = oside[...].reshape(2 * panel, half)
        far = fbufs[h][...].reshape(2 * fbufs[h].shape[1], half)
        last = h == len(chunks) - 1
        to_core(rowwise, 0, w_t * dot_t(fbufs[h][bp], side))
        to_core(rowwise, 1, w_t * dot_t(fbufs[h][1 - bp], side))
        to_cross(rowwise, 0)
        to_core(colwise, 0, w_t * dot_t(oside[1 - bp], far))
        to_cross(rowwise, 1)
        to_core(colwise, 1, w_t * dot_t(oside[bp], far))
        to_cross(colwise, 0)
        to_zed(rowwise, 0, fa)
        to_cross(colwise, 1)
        to_zed(rowwise, 1, fb)
        if last:
            near_tiles()
        to_zed(colwise, 0, near)
        if last:
            to_cross(1, 0)
            to_cross(1, 1)
            to_zed(1, 0, near)

    def finish_cols(h):
        own = summed(3 + 2 * h, 1) + arrived(3 + 2 * h, 0)
        at = 0
        for p in range(2):
            for low, high in chunks[h][1]:
                out_f[:, p * panel + low:p * panel + high] = own[:, at:at + high - low]
                at += high - low

    def finish_rows(h):
        count = chunks[h][0]
        before = sum(chunk[0] for chunk in chunks[:h])
        at = jnp.where(c == 0, before, rows - before - count)
        at = pl.multiple_of(at, 8)
        out_f[pl.ds(at, count)] = out_f[pl.ds(at, count)] + arrived(2 + 2 * h, 0) + arrived(2 + 2 * h, 1)

    near_t.wait_recv()
    left = [near_t]
    for h in range(len(chunks)):
        if h == 0:
            near_t.wait_send()
        if h + 1 < len(chunks):
            widths = [high - low for low, high in chunks[h][1]] * 2
            for copy, width in zip(arriving[h], widths):
                if PACE == 0 or (PACE == 1 and width < max(widths)):
                    copy.wait_send()
                    left.append(copy)
            if h == 0:
                for part in range(len(near_o), 2):
                    send_near(part)
            send_far(h + 1)
        if h == 0:
            to_cross(0, 0)
        far_tiles(h)
    out_d[...] = summed(0, 0)
    for h in range(len(chunks)):
        finish_cols(h)
    for h in range(len(chunks)):
        finish_rows(h)
    out_n[...] = summed(1, 1) + arrived(1, 0)
    for copy in id_copies:
        copy.wait_recv()
    out_ids[...] = idbuf[...]
    for copy in started:
        if not any(copy is other for other in left):
            copy.wait_send()


def two_level_body(gradients, example_ids, lr_weights, checkpoint_order):
    slots, panel, feat = gradients.shape
    half, rows = feat // 2, panel // 4
    vmem = pl.BlockSpec(memory_space=pltpu.VMEM)
    anywhere = pl.BlockSpec(memory_space=pl.ANY)
    chunks = far_chunks(rows)

    def partials(count, height, width):
        return [
            pltpu.VMEM((count, 4, height, width), F32),
            pltpu.VMEM((count, 2, height, width), BF16),
            pltpu.VMEM((count, 2, height, width), BF16),
            *[pltpu.VMEM((count, height, width), BF16)] * 4,
        ]

    scratch = partials(1, rows, panel) + partials(2, rows, panel)
    for count, _ in chunks:
        scratch += partials(2, count, 2 * panel) + partials(2, rows, 8 * count)
    scratch += [pltpu.VMEM((2, 4 * count, half), BF16) for count, _ in chunks]

    d_tile, n_tile, f_tile, col_ids = pl.pallas_call(
        kernel,
        out_shape=[
            jax.ShapeDtypeStruct((rows, panel), F32),
            jax.ShapeDtypeStruct((rows, panel), F32),
            jax.ShapeDtypeStruct((rows, 2 * panel), F32),
            jax.ShapeDtypeStruct((4, 1, panel), jnp.int32),
        ],
        in_specs=[anywhere] * 4,
        out_specs=[vmem] * 4,
        scratch_shapes=[
            pltpu.SMEM(lr_weights.shape, F32),
            pltpu.SMEM(checkpoint_order.shape, jnp.int32),
            pltpu.VMEM((slots, panel, feat), BF16),
            pltpu.VMEM((2, panel, half), BF16),
            pltpu.VMEM((panel, half), BF16),
            pltpu.VMEM((4, 1, panel), jnp.int32),
            pltpu.SemaphoreType.DMA((COPIES,)),
            pltpu.SemaphoreType.DMA((COPIES,)),
            pltpu.SemaphoreType.DMA((5,)),
            *scratch,
        ],
        compiler_params=pltpu.CompilerParams(
            collective_id=0, has_side_effects=True, vmem_limit_bytes=60 * 1024 * 1024
        ),
    )(gradients, example_ids.reshape(1, panel), lr_weights, checkpoint_order)

    b = lax.axis_index("blk")
    side = jnp.where(
        lax.rem(b, 2) == 0,
        jnp.concatenate([d_tile, n_tile], axis=1),
        jnp.concatenate([n_tile, d_tile], axis=1),
    )
    totals = jnp.where(
        b < 2,
        jnp.concatenate([side, f_tile], axis=1),
        jnp.concatenate([f_tile, side], axis=1),
    )
    row_ids = lax.dynamic_slice_in_dim(example_ids, lax.axis_index("dim") * rows, rows)
    same = row_ids[:, None] == col_ids.reshape(1, 4 * panel)
    return jnp.where(same, jnp.float32(0.0), totals)


def solution(mesh):
    fits = mesh.shape["blk"] == 4 and mesh.shape["dim"] == 4
    return jax.shard_map(
        two_level_body if fits else ring_body,
        mesh=mesh,
        in_specs=(P(None, ("groups", "blk"), "dim"), P(("groups", "blk")), P(), P()),
        out_specs=P(("groups", "blk", "dim"), None),
        check_vma=False,
    )
```

```python
import functools

import jax
import jax.numpy as jnp
from jax import lax
from jax.experimental import pallas as pl
from jax.experimental.pallas import tpu as pltpu
from jax.sharding import PartitionSpec as P

F32, BF16 = jnp.float32, jnp.bfloat16


def passed_along(value, axis, steps):
    count = lax.axis_size(axis)
    pairs = [(source, (source + steps) % count) for source in range(count)]
    return lax.ppermute(value, axis, pairs)


def tile_term(local, remote, weights):
    products = lax.dot_general(
        local, remote, (((2,), (2,)), ((0,), (0,))), preferred_element_type=jnp.float32
    )
    return jnp.sum(weights[:, None, None] * products, axis=0).astype(jnp.bfloat16)


def place(totals, col_ids, block, ids, anchor, panel, nblk):
    start = jnp.mod(anchor, nblk) * panel
    totals = lax.dynamic_update_slice(totals, block, (jnp.int32(0), start))
    col_ids = lax.dynamic_update_slice(col_ids, ids.astype(jnp.int32), (start,))
    return (totals, col_ids)


def ring_body(gradients, example_ids, lr_weights, checkpoint_order):
    slots = gradients.shape[0]
    panel = gradients.shape[1]
    nblk = lax.axis_size("blk")
    ndim = lax.axis_size("dim")
    rows = panel // ndim
    whole = panel * nblk
    slot_index = jnp.arange(slots, dtype=jnp.int32)
    weights = jnp.sum(
        jnp.where(
            checkpoint_order[:, None] == slot_index[None, :], lr_weights[None, :], jnp.float32(0.0)
        ),
        axis=1,
    )
    mine = lax.axis_index("blk")
    totals = jnp.zeros((rows, whole), jnp.float32)
    col_ids = jnp.zeros((whole,), jnp.int32)

    def direct(remote):
        return lax.psum_scatter(
            tile_term(gradients, remote, weights), "dim", scatter_dimension=0, tiled=True
        ).astype(jnp.float32)

    totals, col_ids = place(totals, col_ids, direct(gradients), example_ids, mine, panel, nblk)

    def advance(step, carry):
        current, current_ids, totals, col_ids = carry
        current, current_ids = passed_along((current, current_ids), "blk", 1)
        totals, col_ids = place(
            totals, col_ids, direct(current), current_ids, mine - step, panel, nblk
        )
        return (current, current_ids, totals, col_ids)

    carry = lax.fori_loop(1, nblk, advance, (gradients, example_ids, totals, col_ids))
    totals, col_ids = (carry[2], carry[3])
    row_ids = lax.dynamic_slice_in_dim(example_ids, lax.axis_index("dim") * rows, rows)
    same = row_ids[:, None] == col_ids[None, :]
    return jnp.where(same, jnp.float32(0.0), totals)


BOUNDS = (24,)
EARLY = True
PACE = 1
COPIES = 96


def far_chunks(rows):
    chunks, outer = [], rows
    for inner in (*BOUNDS, 0):
        ranges = []
        for pair in range(2):
            middle = (2 * pair + 1) * rows
            if inner:
                ranges += [(middle - outer, middle - inner), (middle + inner, middle + outer)]
            else:
                ranges += [(middle - outer, middle + outer)]
        merged = []
        for low, high in ranges:
            if merged and merged[-1][1] == low:
                merged[-1] = (merged[-1][0], high)
            else:
                merged.append((low, high))
        chunks.append((outer - inner, merged))
        outer = inner
    return chunks


def dot_t(a, b):
    return lax.dot_general(a, b, (((1,), (1,)), ((), ())), preferred_element_type=F32)


def kernel(
    g, ids, lr_in, order_in, out_d, out_n, out_f, out_ids,
    lr, order, gv, oside, near2, idbuf, send, recv, local, *scratch,
):
    b, d = lax.axis_index("blk"), lax.axis_index("dim")
    bp, ct = lax.rem(b, 2), b // 2
    near = b + 1 - 2 * bp
    fa, fb = lax.rem(b + 2, 4), lax.rem(near + 2, 4)
    c, x = lax.rem(d, 2), d // 2
    core, cross = d + 1 - 2 * c, lax.rem(d + 2, 4)
    panel, feat = g.shape[1], g.shape[2]
    half, rows = feat // 2, panel // 4
    chunks = far_chunks(rows)
    groups = [scratch[7 * k:7 * k + 7] for k in range(2 + 2 * len(chunks))]
    fbufs = scratch[7 * len(groups):]

    def cols(p):
        return pl.ds(pl.multiple_of(p * half, 128), half)

    loads = [
        pltpu.make_async_copy(g, gv, local.at[0]),
        pltpu.make_async_copy(g.at[ct, :, cols(bp)], oside.at[bp], local.at[1]),
        pltpu.make_async_copy(ids, idbuf.at[b], local.at[2]),
        pltpu.make_async_copy(lr_in, lr, local.at[3]),
        pltpu.make_async_copy(order_in, order, local.at[4]),
    ]

    barrier = pltpu.get_barrier_semaphore()
    for target in ({"blk": near}, {"blk": fa}, {"blk": fb}, {"dim": core}, {"dim": cross}):
        pl.semaphore_signal(barrier, inc=1, device_id=target, device_id_type=pl.DeviceIdType.MESH)
    pl.semaphore_wait(barrier, 5)

    started = []

    def remote(src, dst, target):
        k = len(started)
        copy = pltpu.make_async_remote_copy(
            src_ref=src, dst_ref=dst, send_sem=send.at[k], recv_sem=recv.at[k],
            device_id=target, device_id_type=pl.DeviceIdType.MESH,
        )
        copy.start()
        started.append(copy)
        return copy

    arriving = []

    def send_far(h):
        count, ranges = chunks[h]
        flight = []
        for to, p in ((fb, 1 - bp), (fa, bp)):
            place_at = 0
            for low, high in ranges:
                flight.append(remote(
                    g.at[1 - ct, pl.ds(low, high - low), cols(p)],
                    fbufs[h].at[bp, pl.ds(place_at, high - low)],
                    {"blk": to},
                ))
                place_at += high - low
        arriving.append(flight)

    send_far(0)
    near_t = remote(g.at[ct, :, cols(1 - bp)], oside.at[bp], {"blk": near})
    near_o = []

    def send_near(part):
        piece = pl.ds(part * 2 * rows, 2 * rows)
        near_o.append(remote(g.at[1 - ct, piece, cols(1 - bp)], near2.at[piece], {"blk": near}))

    if EARLY:
        send_near(0)
        send_near(1)
    for load in loads:
        load.start()
    for load in loads:
        load.wait()
    id_copies = [remote(idbuf.at[b], idbuf.at[b], {"blk": to}) for to in (near, fa, fb)]

    def weight(slot):
        total = jnp.float32(0.0)
        for k in range(lr.shape[0]):
            total = total + jnp.where(order[slot] == k, lr[k], jnp.float32(0.0))
        return total

    w0, w1 = weight(0), weight(1)
    w_t = jnp.where(ct == 0, w0, w1)
    w_o = jnp.where(ct == 0, w1, w0)
    flight = {}

    def to_core(grp, i, value):
        acc, cs, cr = groups[grp][:3]
        height = acc.shape[2]
        for q in range(4):
            acc[i, q] = value[q * height:(q + 1) * height]
        for q in range(2):
            cs[i, q] = acc[i, 2 * q + 1 - c].astype(BF16)
        flight[grp, i, 0] = remote(cs.at[i], cr.at[i], {"dim": core})

    def to_cross(grp, i):
        acc, _, cr, xs, xr = groups[grp][:5]
        flight[grp, i, 0].wait_recv()
        y = 1 - x
        xs[i] = (acc[i, 2 * y + c] + cr[i, y].astype(F32)).astype(BF16)
        flight[grp, i, 1] = remote(xs.at[i], xr.at[i], {"dim": cross})

    def summed(grp, i):
        acc, _, cr, _, xr = groups[grp][:5]
        flight[grp, i, 1].wait_recv()
        return acc[i, 2 * x + c] + cr[i, x].astype(F32) + xr[i].astype(F32)

    def to_zed(grp, i, to):
        zs, zr = groups[grp][5:]
        zs[i] = summed(grp, i).astype(BF16)
        flight[grp, i, 2] = remote(zs.at[i], zr.at[i], {"blk": to})

    def arrived(grp, i):
        flight[grp, i, 2].wait_recv()
        return groups[grp][6][i].astype(F32)

    to_core(0, 0, w0 * dot_t(gv[0], gv[0]) + w1 * dot_t(gv[1], gv[1]))

    def near_tiles():
        for copy in near_o:
            copy.wait_recv()
        own2 = gv[1 - ct, :, cols(bp)]
        to_core(1, 0, w_t * dot_t(oside[1 - bp], oside[bp]) + w_o * dot_t(near2[...], own2))
        to_core(1, 1, w_t * dot_t(oside[bp], oside[1 - bp]) + w_o * dot_t(own2, near2[...]))
    def far_tiles(h):
        rowwise, colwise = 2 + 2 * h, 3 + 2 * h
        for copy in arriving[h]:
            copy.wait_recv()
        side = oside[...].reshape(2 * panel, half)
        far = fbufs[h][...].reshape(2 * fbufs[h].shape[1], half)
        last = h == len(chunks) - 1
        to_core(rowwise, 0, w_t * dot_t(fbufs[h][bp], side))
        to_core(rowwise, 1, w_t * dot_t(fbufs[h][1 - bp], side))
        to_cross(rowwise, 0)
        to_core(colwise, 0, w_t * dot_t(oside[1 - bp], far))
        to_cross(rowwise, 1)
        to_core(colwise, 1, w_t * dot_t(oside[bp], far))
        to_cross(colwise, 0)
        to_zed(rowwise, 0, fa)
        to_cross(colwise, 1)
        to_zed(rowwise, 1, fb)
        to_zed(colwise, 0, near)

    def finish_cols(h):
        own = summed(3 + 2 * h, 1) + arrived(3 + 2 * h, 0)
        at = 0
        for p in range(2):
            for low, high in chunks[h][1]:
                out_f[:, p * panel + low:p * panel + high] = own[:, at:at + high - low]
                at += high - low

    def finish_rows(h):
        count = chunks[h][0]
        before = sum(chunk[0] for chunk in chunks[:h])
        at = jnp.where(c == 0, before, rows - before - count)
        at = pl.multiple_of(at, 8)
        out_f[pl.ds(at, count)] = out_f[pl.ds(at, count)] + arrived(2 + 2 * h, 0) + arrived(2 + 2 * h, 1)

    near_t.wait_recv()
    left = [near_t]
    for h in range(len(chunks)):
        if h == 0:
            near_t.wait_send()
        if h + 1 < len(chunks):
            widths = [high - low for low, high in chunks[h][1]] * 2
            for copy, width in zip(arriving[h], widths):
                if PACE == 0 or (PACE == 1 and width < max(widths)):
                    copy.wait_send()
                    left.append(copy)
            if h == 0:
                for part in range(len(near_o), 2):
                    send_near(part)
            send_far(h + 1)
        if h == 0:
            to_cross(0, 0)
        if h == len(chunks) - 1:
            near_tiles()
            to_cross(1, 0)
            to_cross(1, 1)
            to_zed(1, 0, near)
        far_tiles(h)
    out_d[...] = summed(0, 0)
    for h in range(len(chunks)):
        finish_cols(h)
    for h in range(len(chunks)):
        finish_rows(h)
    out_n[...] = summed(1, 1) + arrived(1, 0)
    for copy in id_copies:
        copy.wait_recv()
    out_ids[...] = idbuf[...]
    for copy in started:
        if not any(copy is other for other in left):
            copy.wait_send()


def two_level_body(gradients, example_ids, lr_weights, checkpoint_order):
    slots, panel, feat = gradients.shape
    half, rows = feat // 2, panel // 4
    vmem = pl.BlockSpec(memory_space=pltpu.VMEM)
    anywhere = pl.BlockSpec(memory_space=pl.ANY)
    chunks = far_chunks(rows)

    def partials(count, height, width):
        return [
            pltpu.VMEM((count, 4, height, width), F32),
            pltpu.VMEM((count, 2, height, width), BF16),
            pltpu.VMEM((count, 2, height, width), BF16),
            *[pltpu.VMEM((count, height, width), BF16)] * 4,
        ]

    scratch = partials(1, rows, panel) + partials(2, rows, panel)
    for count, _ in chunks:
        scratch += partials(2, count, 2 * panel) + partials(2, rows, 8 * count)
    scratch += [pltpu.VMEM((2, 4 * count, half), BF16) for count, _ in chunks]

    d_tile, n_tile, f_tile, col_ids = pl.pallas_call(
        kernel,
        out_shape=[
            jax.ShapeDtypeStruct((rows, panel), F32),
            jax.ShapeDtypeStruct((rows, panel), F32),
            jax.ShapeDtypeStruct((rows, 2 * panel), F32),
            jax.ShapeDtypeStruct((4, 1, panel), jnp.int32),
        ],
        in_specs=[anywhere] * 4,
        out_specs=[vmem] * 4,
        scratch_shapes=[
            pltpu.SMEM(lr_weights.shape, F32),
            pltpu.SMEM(checkpoint_order.shape, jnp.int32),
            pltpu.VMEM((slots, panel, feat), BF16),
            pltpu.VMEM((2, panel, half), BF16),
            pltpu.VMEM((panel, half), BF16),
            pltpu.VMEM((4, 1, panel), jnp.int32),
            pltpu.SemaphoreType.DMA((COPIES,)),
            pltpu.SemaphoreType.DMA((COPIES,)),
            pltpu.SemaphoreType.DMA((5,)),
            *scratch,
        ],
        compiler_params=pltpu.CompilerParams(
            collective_id=0, has_side_effects=True, vmem_limit_bytes=60 * 1024 * 1024
        ),
    )(gradients, example_ids.reshape(1, panel), lr_weights, checkpoint_order)

    b = lax.axis_index("blk")
    side = jnp.where(
        lax.rem(b, 2) == 0,
        jnp.concatenate([d_tile, n_tile], axis=1),
        jnp.concatenate([n_tile, d_tile], axis=1),
    )
    totals = jnp.where(
        b < 2,
        jnp.concatenate([side, f_tile], axis=1),
        jnp.concatenate([f_tile, side], axis=1),
    )
    row_ids = lax.dynamic_slice_in_dim(example_ids, lax.axis_index("dim") * rows, rows)
    same = row_ids[:, None] == col_ids.reshape(1, 4 * panel)
    return jnp.where(same, jnp.float32(0.0), totals)


def solution(mesh):
    fits = mesh.shape["blk"] == 4 and mesh.shape["dim"] == 4
    return jax.shard_map(
        two_level_body if fits else ring_body,
        mesh=mesh,
        in_specs=(P(None, ("groups", "blk"), "dim"), P(("groups", "blk")), P(), P()),
        out_specs=P(("groups", "blk", "dim"), None),
        check_vma=False,
    )
```
